512 devices in a mesh: dp: 32 (over y, z_lo, core), tensor: 16 (over x, z_hi).
Axes of the slice: x: 4, y: 8, z: 8 (z_hi: 4, z_lo: 2; z = z_hi * 2 + z_lo), core: 2. Of those that a mesh axis runs over, the one named last changes fastest.
Arguments:
- tokens: bfloat16 [1024, 4096], P('dp', 'tensor'), may hold values from -6 to 6
- cotangent: bfloat16 [1024, 4096], P('dp', 'tensor'), may hold values from -0.011962891 to 0.011962891
- gate_rows: bfloat16 [6, 14336, 4096], P(None, ('dp', 'tensor')), may hold values from -0.09375 to 0.09375
- up_rows: bfloat16 [6, 14336, 4096], P(None, ('dp', 'tensor')), may hold values from -0.09375 to 0.09375
- down_rows: bfloat16 [6, 14336, 4096], P(None, ('dp', 'tensor')), may hold values from -0.046875 to 0.046875
- router_logits: float32 [8, 6], replicated, may hold values from -12 to 260
Outputs:
- merge_grad: float32 [8, 6], replicated
- router_grad: float32 [8, 6], replicated
The draws below stay inside these ranges and needn't reach their ends.
All inputs are finite; a program needn't handle non-finite values.
Results may differ from the reference program's by a relative error of at most 0.0005.
Values may be sent and summed in bfloat16 or wider, within the bound.
No kernel may reach another device: no remote copies, remote signals or barrier semaphores. Data moves between devices by JAX's collectives and lax.ppermute only.
A program may use at most 64 MiB of HBM per device.

```python
import jax
import jax.numpy as jnp
from jax import lax

D = 4096
FF = 14336
E = 6
SEG = 128
TOKENS = 1024
SEGS = 8


def draw_router_logits(key, part):
    key = jax.random.fold_in(key, 7)
    key_list = jax.random.split(key, 1)
    base_draw = jnp.clip(2.0 * jax.random.normal(key_list[0], (SEGS, E), jnp.float32), -12.0, 12.0)
    return base_draw


def block_scale(own_key, dims, pieces, low, largest):
    def one(axis_at, parts):
        steps = jax.random.uniform(jax.random.fold_in(jax.random.fold_in(own_key, 6), axis_at), (parts,), jnp.float32, low / len(pieces), largest / len(pieces))
        return jnp.repeat(jnp.exp(steps), dims[axis_at] // parts).reshape((-1,) + (1,) * (len(dims) - axis_at - 1))

    level = one(*pieces[0])
    for cut in pieces[1:]:
        level = level * one(*cut)
    return level


def gaussian(key, extent, spread, limit, cuts=(), kind=jnp.bfloat16):
    drawn = spread * jax.random.normal(key, extent, jnp.float32)
    if cuts:
        drawn = drawn * block_scale(key, extent, cuts, -0.22, 0.18)
    return jnp.clip(drawn, -limit, limit).astype(kind)


def setup_inputs(seed: int = 0) -> dict:
    arg_keys = jax.random.split(jax.random.key(seed), 7)
    tokens = gaussian(arg_keys[0], (TOKENS, D), 1.0, 6.0, ((0, 32), (1, 16)))
    cotangent = gaussian(arg_keys[1], (TOKENS, D), 0.002, 0.011962891, ((0, 32), (1, 16)))
    gate_rows = gaussian(arg_keys[2], (E, FF, D), D ** -0.5, 0.09375, ((1, 512),))
    up_rows = gaussian(arg_keys[3], (E, FF, D), D ** -0.5, 0.09375, ((1, 512),))
    down_rows = gaussian(arg_keys[4], (E, FF, D), FF ** -0.5, 0.046875, ((1, 512),))
    router_logits = draw_router_logits(jax.random.fold_in(arg_keys[6], 71), 0)
    return dict(tokens=tokens, cotangent=cotangent, gate_rows=gate_rows, up_rows=up_rows, down_rows=down_rows, router_logits=router_logits)


def token_terms(projected, mixing_rows):
    highest = lax.Precision.HIGHEST
    gate_sum = jnp.einsum("et,eft->ft", mixing_rows, projected[0], precision=highest)
    upward = jnp.einsum("et,eft->ft", mixing_rows, projected[1], precision=highest)
    backward = jnp.einsum("et,eft->ft", mixing_rows, projected[2], precision=highest)
    sigmoid_gate = jax.nn.sigmoid(gate_sum)
    active = gate_sum * sigmoid_gate
    hidden = active * upward
    grad_gate = backward * upward * sigmoid_gate * (1.0 + gate_sum * (1.0 - sigmoid_gate))
    grad_up = backward * active
    return (jnp.einsum("ft,eft->et", grad_gate, projected[0], precision=highest)
            + jnp.einsum("ft,eft->et", grad_up, projected[1], precision=highest)
            + jnp.einsum("ft,eft->et", hidden, projected[2], precision=highest))


def reference(tokens, cotangent, gate_rows, up_rows, down_rows, router_logits):
    highest = lax.Precision.HIGHEST
    mixing = jax.nn.softmax(router_logits, axis=-1)
    position = jnp.arange(tokens.shape[0], dtype=jnp.int32) // SEG
    seg_table = (jnp.arange(SEGS, dtype=jnp.int32)[:, None] == position[None, :]).astype(jnp.float32)
    mixing_rows = jnp.dot(mixing.T, seg_table, precision=highest)

    def project(expert):
        return jnp.stack([
            jnp.dot(gate_rows[expert], tokens.T, preferred_element_type=jnp.float32),
            jnp.dot(up_rows[expert], tokens.T, preferred_element_type=jnp.float32),
            jnp.dot(down_rows[expert], cotangent.T, preferred_element_type=jnp.float32)])

    projected = jnp.moveaxis(lax.map(project, jnp.arange(E, dtype=jnp.int32)), 1, 0)
    token_sums = token_terms(projected, mixing_rows)
    merge_grad = jnp.dot(seg_table, token_sums.T, precision=highest)
    router_grad = mixing * (merge_grad - jnp.sum(mixing * merge_grad, axis=-1, keepdims=True))
    return merge_grad, router_grad
```

```python
import functools

import jax
import jax.numpy as jnp
from jax import lax
from jax.experimental import pallas as pl
from jax.experimental.pallas import tpu as pltpu
from jax.sharding import Mesh, PartitionSpec as P

E = 6
HID = 28
PAD = 32
D = 4096
ROWS = 32
FEATS = 256
RING = 8
SIZES = {"y": 8, "zl": 2, "c": 2, "x": 4, "zh": 4}
OFFSETS = (0, -1, 1, -2, 2, -3, 3, 4)
HIGHEST = lax.Precision.HIGHEST


def gather_by_exchange(block, axes):
    members = 1
    for axis in axes:
        members *= SIZES[axis]
    copies = jnp.broadcast_to(block[None], (members,) + block.shape)
    return lax.all_to_all(copies, axes, 0, 0)


def y_shift(block, step):
    return lax.ppermute(block, "y", [(i, (i + step) % 8) for i in range(8)])


def z_place(z):
    z %= 8
    return (z % 2) * 4 + z // 2


def z_shift(block, step):
    return lax.ppermute(
        block, ("zl", "zh"), [(z_place(z), z_place(z + step)) for z in range(8)]
    )


def rings(firsts, shifts):
    moving = [(first, first) for first in firsts]
    found = [[first] for first in firsts]
    for _ in range(RING // 2 - 1):
        moving = [
            (shift(up, 1), shift(down, -1)) for shift, (up, down) in zip(shifts, moving)
        ]
        for blocks, pair in zip(found, moving):
            blocks += pair
    for blocks, shift, (up, down) in zip(found, shifts, moving):
        half = up.shape[0] // 2
        blocks += [shift(up[:half], 1), shift(down[half:], -1)]
    return found


def compute_kernel(place_ref, mix_ref, *refs):
    own, other = refs[0:3], refs[3:6]
    a_refs, b_refs = refs[6:15], refs[15:24]
    out_ref = refs[24]
    w_ref, tok_ref, cot_ref, acc_ref = refs[25:]
    my_y, my_z = place_ref[0], place_ref[1]

    for m in range(3):
        for p, source in enumerate((own, other)):
            for e in range(E):
                w_ref[m, p * E + e, 16:PAD, :] = jnp.zeros((PAD - 16, D), jnp.bfloat16)
                w_ref[m, p * E + e, 0:HID, :] = source[m][e]

    for k in range(8):
        for zl in range(2):
            for t in range(16):
                if k < 7:
                    piece = a_refs[k][zl * 16 + t]
                else:
                    piece = a_refs[7 + zl][t]
                tok_ref[zl, k * ROWS:(k + 1) * ROWS, t * FEATS:(t + 1) * FEATS] = piece
    for j in range(8):
        z = lax.rem(my_z + OFFSETS[j] + 8, 8)
        for x in range(4):
            for k in range(8):
                y = lax.rem(my_y + OFFSETS[k] + 8, 8)
                if j < 7:
                    piece = b_refs[j][x * 8 + y]
                else:
                    piece = b_refs[7 + x // 2][(x % 2) * 8 + y]
                cot_ref[z, k * ROWS:(k + 1) * ROWS, x * FEATS:(x + 1) * FEATS] = piece

    dims = (((1,), (1,)), ((), ()))
    for zl in range(2):
        for m in range(2):
            def project(i, _, zl=zl, m=m):
                rows = w_ref[m, pl.ds(i * 6, 6)].reshape(6 * PAD, D)
                got = lax.dot_general(rows, tok_ref[zl], dims, preferred_element_type=jnp.float32)
                acc_ref[m, zl, pl.ds(i * 6, 6)] = got.reshape(6, PAD, 256)
                return 0
            lax.fori_loop(0, 2, project, 0)

        def project_back(i, _, zl=zl):
            total = jnp.zeros((6 * PAD, 256), jnp.float32)
            for zh in range(4):
                rows = jnp.concatenate(
                    [w_ref[2, pl.ds(i * 6, 6), :, (x * 4 + zh) * FEATS:(x * 4 + zh + 1) * FEATS] for x in range(4)],
                    axis=-1,
                ).reshape(6 * PAD, 4 * FEATS)
                total += lax.dot_general(rows, cot_ref[zh * 2 + zl], dims, preferred_element_type=jnp.float32)
            acc_ref[2, zl, pl.ds(i * 6, 6)] = total.reshape(6, PAD, 256)
            return 0
        lax.fori_loop(0, 2, project_back, 0)

    mix = [mix_ref[e:e + 1, :] for e in range(E)]
    sums = [jnp.zeros((8, 256), jnp.float32) for _ in range(E)]
    for zl in range(2):
        for p in range(2):
            for r in range(PAD // 8):
                rows = pl.ds(r * 8, 8)
                gate = [acc_ref[0, zl, p * E + e, rows, :] for e in range(E)]
                up = [acc_ref[1, zl, p * E + e, rows, :] for e in range(E)]
                back = [acc_ref[2, zl, p * E + e, rows, :] for e in range(E)]
                gate_sum = sum(mix[e] * gate[e] for e in range(E))
                upward = sum(mix[e] * up[e] for e in range(E))
                backward = sum(mix[e] * back[e] for e in range(E))
                sigmoid = jax.nn.sigmoid(gate_sum)
                active = gate_sum * sigmoid
                hidden = active * upward
                grad_gate = backward * upward * sigmoid * (1.0 + gate_sum * (1.0 - sigmoid))
                grad_up = backward * active
                for e in range(E):
                    sums[e] += grad_gate * gate[e] + grad_up * up[e] + hidden * back[e]
    token_sums = [jnp.sum(sums[e], axis=0, keepdims=True) for e in range(E)]
    lane = lax.broadcasted_iota(jnp.int32, (8, 256), 1)
    seg = lax.broadcasted_iota(jnp.int32, (8, 256), 0)
    lane_seg = jnp.zeros((8, 256), jnp.int32)
    for k in range(8):
        y = lax.rem(my_y + OFFSETS[k] + 8, 8)
        lane_seg = jnp.where(lane // ROWS == k, y, lane_seg)
    belongs = lane_seg == seg
    out_lane = lax.broadcasted_iota(jnp.int32, (8, 128), 1)
    out = jnp.zeros((8, 128), jnp.float32)
    for e in range(E):
        column = jnp.sum(jnp.where(belongs, token_sums[e], 0.0), axis=1, keepdims=True)
        out = jnp.where(out_lane == e, column, out)
    out_ref[...] = jnp.broadcast_to(out[None], out_ref.shape)


def add_kernel(got_ref, out_ref):
    out_ref[...] = jnp.broadcast_to(jnp.sum(got_ref[...], axis=0)[None], out_ref.shape)


def finish_kernel(got_ref, logits_ref, merge_ref, router_ref):
    merge_grad = jnp.sum(got_ref[...], axis=0)[:, :E]
    logits = logits_ref[...]
    raised = jnp.exp(logits - jnp.max(logits, axis=-1, keepdims=True))
    mixing = raised / jnp.sum(raised, axis=-1, keepdims=True)
    merge_ref[...] = merge_grad
    router_ref[...] = mixing * (
        merge_grad - jnp.sum(mixing * merge_grad, axis=-1, keepdims=True)
    )


VMEM = pl.BlockSpec(memory_space=pltpu.VMEM)
SMEM = pl.BlockSpec(memory_space=pltpu.SMEM)


def on_device(tokens, cotangent, gate_rows, up_rows, down_rows, router_logits):
    my_y = lax.axis_index("y")
    my_z = lax.axis_index("zh") * 2 + lax.axis_index("zl")
    mine = (gate_rows, up_rows, down_rows)
    theirs = [lax.ppermute(w, "c", [(0, 1), (1, 0)]) for w in mine]
    a_first = gather_by_exchange(tokens, ("zl", "x", "zh"))
    b_first = gather_by_exchange(cotangent, ("x", "y"))
    a_blocks, b_blocks = rings((a_first, b_first), (y_shift, z_shift))

    mixing = jax.nn.softmax(router_logits, axis=-1)
    order = jnp.array([(o + 8) % 8 for o in OFFSETS], jnp.int32)
    mix_rows = jnp.repeat(jnp.take(mixing, (order + my_y) % 8, axis=0), ROWS, axis=0).T
    mix_rows = jnp.pad(mix_rows, ((0, 2), (0, 0)))
    place = jnp.stack([my_y, my_z]).astype(jnp.int32)
    part = pl.pallas_call(
        compute_kernel,
        out_shape=jax.ShapeDtypeStruct((32, 8, 128), jnp.float32),
        in_specs=[SMEM, VMEM] + [VMEM] * 24,
        out_specs=VMEM,
        scratch_shapes=[
            pltpu.VMEM((3, 2 * E, PAD, D), jnp.bfloat16),
            pltpu.VMEM((2, 256, D), jnp.bfloat16),
            pltpu.VMEM((8, 256, 4 * FEATS), jnp.bfloat16),
            pltpu.VMEM((3, 2, 2 * E, PAD, 256), jnp.float32),
        ],
        compiler_params=pltpu.CompilerParams(vmem_limit_bytes=60 * 1024 * 1024),
    )(place, mix_rows, *mine, *theirs, *a_blocks, *b_blocks)
    got = lax.all_to_all(part, ("x", "y"), 0, 0)
    part = pl.pallas_call(
        add_kernel,
        out_shape=jax.ShapeDtypeStruct((16, 8, 128), jnp.float32),
        in_specs=[VMEM],
        out_specs=VMEM,
    )(got)
    got = lax.all_to_all(part, ("zl", "c", "zh"), 0, 0)
    small = jax.ShapeDtypeStruct((8, E), jnp.float32)
    return pl.pallas_call(
        finish_kernel,
        out_shape=(small, small),
        in_specs=[VMEM, VMEM],
        out_specs=(VMEM, VMEM),
    )(got, router_logits)


def solution(mesh):
    fine = Mesh(mesh.devices.reshape(8, 2, 2, 4, 4), ("y", "zl", "c", "x", "zh"))
    dp, tensor = ("y", "zl", "c"), ("x", "zh")
    weights = P(None, dp + tensor, None)
    return jax.shard_map(
        on_device,
        mesh=fine,
        in_specs=(P(dp, tensor), P(dp, tensor), weights, weights, weights, P()),
        out_specs=(P(), P()),
        check_vma=False,
    )
```

```python
import itertools

import jax
import jax.numpy as jnp
from jax import lax
from jax.experimental import pallas as pl
from jax.experimental.pallas import tpu as pltpu
from jax.sharding import Mesh, PartitionSpec as P

E = 6
HID = 28
PAD = 32
D = 4096
ROWS = 32
FEATS = 256
RING = 8
ALL = ("y", "zl", "c", "x", "zh")
OFFSETS = (0, -1, 1, -2, 2, -3, 3, 4)


def device(y, z, core, x):
    y, z = y % 8, z % 8
    return (((y * 2 + z % 2) * 2 + core) * 4 + x) * 4 + z // 2


PLACES = tuple(itertools.product(range(8), range(8), range(2), range(4)))


def shift(block, axis, step):
    pairs = []
    for y, z, core, x in PLACES:
        go = step if core == 0 else -step
        to = (y + go, z, core, x) if axis == "y" else (y, z + go, core, x)
        pairs.append((device(y, z, core, x), device(*to)))
    return lax.ppermute(block, ALL, pairs)


def swap_cores(block):
    return lax.ppermute(block, "c", [(0, 1), (1, 0)])


def plane_groups():
    first = [
        [device(y, zl + 2 * zh, 0, x) for zl in range(2) for x in range(4) for zh in range(4)]
        for y in range(8)
    ]
    second = [[device(y, z, 1, x) for x in range(4) for y in range(8)] for z in range(8)]
    return first + second


def rings(a, b):
    a_fore = a_back = a
    b_fore = b_back = b
    a_blocks, b_blocks = [a], [b]
    for _ in range(RING // 2 - 1):
        a_fore, b_fore = shift(a_fore, "y", 1), shift(b_fore, "z", 1)
        a_back, b_back = shift(a_back, "y", -1), shift(b_back, "z", -1)
        a_blocks += [a_fore, a_back]
        b_blocks += [b_fore, b_back]
    a_blocks.append(shift(a_fore, "y", 1))
    b_blocks.append(shift(b_fore, "z", 1))
    return a_blocks, b_blocks


def compute_kernel(place_ref, mix_ref, *refs):
    own, other = refs[0:3], refs[3:6]
    a_refs, b_refs = refs[6:14], refs[14:22]
    out_ref = refs[22]
    w_ref, tok_ref, cot_ref, acc_ref = refs[23:]
    my_y, my_z, sign = place_ref[0], place_ref[1], place_ref[2]

    for m in range(3):
        for p, source in enumerate((own, other)):
            for e in range(E):
                w_ref[m, p * E + e, 16:PAD, :] = jnp.zeros((PAD - 16, D), jnp.bfloat16)
                w_ref[m, p * E + e, 0:HID, :] = source[m][e]

    for k in range(8):
        for zl in range(2):
            for t in range(16):
                piece = a_refs[k][zl * 16 + t]
                tok_ref[zl, k * ROWS:(k + 1) * ROWS, t * FEATS:(t + 1) * FEATS] = piece
    for j in range(8):
        z = lax.rem(my_z + sign * OFFSETS[j] + 8, 8)
        for x in range(4):
            for k in range(8):
                y = lax.rem(my_y + sign * OFFSETS[k] + 8, 8)
                piece = b_refs[j][x * 8 + y]
                cot_ref[z, k * ROWS:(k + 1) * ROWS, x * FEATS:(x + 1) * FEATS] = piece

    dims = (((1,), (1,)), ((), ()))
    for zl in range(2):
        for m in range(2):
            def project(i, _, zl=zl, m=m):
                rows = w_ref[m, pl.ds(i * 6, 6)].reshape(6 * PAD, D)
                got = lax.dot_general(rows, tok_ref[zl], dims, preferred_element_type=jnp.float32)
                acc_ref[m, zl, pl.ds(i * 6, 6)] = got.reshape(6, PAD, 256)
                return 0
            lax.fori_loop(0, 2, project, 0)

        def project_back(i, _, zl=zl):
            total = jnp.zeros((6 * PAD, 256), jnp.float32)
            for zh in range(4):
                rows = jnp.concatenate(
                    [w_ref[2, pl.ds(i * 6, 6), :, (x * 4 + zh) * FEATS:(x * 4 + zh + 1) * FEATS] for x in range(4)],
                    axis=-1,
                ).reshape(6 * PAD, 4 * FEATS)
                total += lax.dot_general(rows, cot_ref[zh * 2 + zl], dims, preferred_element_type=jnp.float32)
            acc_ref[2, zl, pl.ds(i * 6, 6)] = total.reshape(6, PAD, 256)
            return 0
        lax.fori_loop(0, 2, project_back, 0)

    mix = [mix_ref[e:e + 1, :] for e in range(E)]
    sums = [jnp.zeros((8, 256), jnp.float32) for _ in range(E)]
    for zl in range(2):
        for p in range(2):
            for r in range(PAD // 8):
                rows = pl.ds(r * 8, 8)
                gate = [acc_ref[0, zl, p * E + e, rows, :] for e in range(E)]
                up = [acc_ref[1, zl, p * E + e, rows, :] for e in range(E)]
                back = [acc_ref[2, zl, p * E + e, rows, :] for e in range(E)]
                gate_sum = sum(mix[e] * gate[e] for e in range(E))
                upward = sum(mix[e] * up[e] for e in range(E))
                backward = sum(mix[e] * back[e] for e in range(E))
                sigmoid = jax.nn.sigmoid(gate_sum)
                active = gate_sum * sigmoid
                hidden = active * upward
                grad_gate = backward * upward * sigmoid * (1.0 + gate_sum * (1.0 - sigmoid))
                grad_up = backward * active
                for e in range(E):
                    sums[e] += grad_gate * gate[e] + grad_up * up[e] + hidden * back[e]
    token_sums = [jnp.sum(sums[e], axis=0, keepdims=True) for e in range(E)]
    lane = lax.broadcasted_iota(jnp.int32, (8, 256), 1)
    seg = lax.broadcasted_iota(jnp.int32, (8, 256), 0)
    lane_seg = jnp.zeros((8, 256), jnp.int32)
    for k in range(8):
        y = lax.rem(my_y + sign * OFFSETS[k] + 8, 8)
        lane_seg = jnp.where(lane // ROWS == k, y, lane_seg)
    belongs = lane_seg == seg
    out_lane = lax.broadcasted_iota(jnp.int32, (8, 128), 1)
    out = jnp.zeros((8, 128), jnp.float32)
    for e in range(E):
        column = jnp.sum(jnp.where(belongs, token_sums[e], 0.0), axis=1, keepdims=True)
        out = jnp.where(out_lane == e, column, out)
    out_ref[...] = jnp.broadcast_to(out[None], out_ref.shape)


def add_kernel(got_ref, out_ref):
    out_ref[...] = jnp.broadcast_to(jnp.sum(got_ref[...], axis=0)[None], out_ref.shape)


def finish_kernel(got_ref, logits_ref, merge_ref, router_ref):
    merge_grad = jnp.sum(got_ref[...], axis=0)[:, :E]
    logits = logits_ref[...]
    raised = jnp.exp(logits - jnp.max(logits, axis=-1, keepdims=True))
    mixing = raised / jnp.sum(raised, axis=-1, keepdims=True)
    merge_ref[...] = merge_grad
    router_ref[...] = mixing * (
        merge_grad - jnp.sum(mixing * merge_grad, axis=-1, keepdims=True)
    )


VMEM = pl.BlockSpec(memory_space=pltpu.VMEM)
SMEM = pl.BlockSpec(memory_space=pltpu.SMEM)


def on_device(tokens, cotangent, gate_rows, up_rows, down_rows, router_logits):
    my_y = lax.axis_index("y")
    my_z = lax.axis_index("zh") * 2 + lax.axis_index("zl")
    core = lax.axis_index("c")
    sign = 1 - 2 * core
    mine = (gate_rows, up_rows, down_rows)
    keep = jnp.where(core == 0, tokens, cotangent)
    got = swap_cores(jnp.where(core == 0, cotangent, tokens))
    pair = jnp.stack([keep, got])
    plane = lax.all_to_all(
        jnp.broadcast_to(pair[None], (32,) + pair.shape), ALL, 0, 0, axis_index_groups=plane_groups()
    )
    own = plane[:, 0]
    theirs = swap_cores(plane[:, 1])
    a_first = jnp.where(core == 0, own, theirs)
    b_first = jnp.where(core == 0, theirs, own)
    other = [swap_cores(w) for w in mine]
    a_first, b_first, *other = lax.optimization_barrier((a_first, b_first, *other))
    a_blocks, b_blocks = rings(a_first, b_first)

    mixing = jax.nn.softmax(router_logits, axis=-1)
    order = jnp.array(OFFSETS, jnp.int32)
    mix_rows = jnp.repeat(jnp.take(mixing, (sign * order + my_y) % 8, axis=0), ROWS, axis=0).T
    mix_rows = jnp.pad(mix_rows, ((0, 2), (0, 0)))
    place = jnp.stack([my_y, my_z, sign]).astype(jnp.int32)
    part = pl.pallas_call(
        compute_kernel,
        out_shape=jax.ShapeDtypeStruct((32, 8, 128), jnp.float32),
        in_specs=[SMEM, VMEM] + [VMEM] * 22,
        out_specs=VMEM,
        scratch_shapes=[
            pltpu.VMEM((3, 2 * E, PAD, D), jnp.bfloat16),
            pltpu.VMEM((2, 256, D), jnp.bfloat16),
            pltpu.VMEM((8, 256, 4 * FEATS), jnp.bfloat16),
            pltpu.VMEM((3, 2, 2 * E, PAD, 256), jnp.float32),
        ],
        compiler_params=pltpu.CompilerParams(vmem_limit_bytes=60 * 1024 * 1024),
    )(place, mix_rows, *mine, *other, *a_blocks, *b_blocks)
    got = lax.all_to_all(part, ("x", "y"), 0, 0)
    part = pl.pallas_call(
        add_kernel,
        out_shape=jax.ShapeDtypeStruct((16, 8, 128), jnp.float32),
        in_specs=[VMEM],
        out_specs=VMEM,
    )(got)
    got = lax.all_to_all(part, ("zl", "zh", "c"), 0, 0)
    small = jax.ShapeDtypeStruct((8, E), jnp.float32)
    return pl.pallas_call(
        finish_kernel,
        out_shape=(small, small),
        in_specs=[VMEM, VMEM],
        out_specs=(VMEM, VMEM),
    )(got, router_logits)


def solution(mesh):
    fine = Mesh(mesh.devices.reshape(8, 2, 2, 4, 4), ("y", "zl", "c", "x", "zh"))
    dp, tensor = ("y", "zl", "c"), ("x", "zh")
    weights = P(None, dp + tensor, None)
    return jax.shard_map(
        on_device,
        mesh=fine,
        in_specs=(P(dp, tensor), P(dp, tensor), weights, weights, weights, P()),
        out_specs=(P(), P()),
        check_vma=False,
    )
```

```python
import itertools

import jax
import jax.numpy as jnp
from jax import lax
from jax.experimental import pallas as pl
from jax.experimental.pallas import tpu as pltpu
from jax.sharding import Mesh, PartitionSpec as P

E = 6
HID = 28
PAD = 32
D = 4096
ROWS = 32
FEATS = 256
RING = 8
MIB = 1024 * 1024
VMEM = pl.BlockSpec(memory_space=pltpu.VMEM)
SMEM = pl.BlockSpec(memory_space=pltpu.SMEM)
ALL = ("y", "zl", "c", "x", "zh")
OFFSETS = (0, -1, 1, -2, 2, -3, 3, 4)


def device(y, z, core, x):
    y, z = y % 8, z % 8
    return (((y * 2 + z % 2) * 2 + core) * 4 + x) * 4 + z // 2


PLACES = tuple(itertools.product(range(8), range(8), range(2), range(4)))


def shift(block, whose, step):
    pairs = []
    for y, z, core, x in PLACES:
        go = step if core == 0 else -step
        along_y = (core == 0) == (whose == "own")
        to = (y + go, z, core, x) if along_y else (y, z + go, core, x)
        pairs.append((device(y, z, core, x), device(*to)))
    return lax.ppermute(block, ALL, pairs)


def swap_cores(block):
    return lax.ppermute(block, "c", [(0, 1), (1, 0)])


def plane_groups():
    first = [
        [device(y, zl + 2 * zh, 0, x) for zl in range(2) for x in range(4) for zh in range(4)]
        for y in range(8)
    ]
    second = [[device(y, z, 1, x) for x in range(4) for y in range(8)] for z in range(8)]
    return first + second


def rings(own, theirs):
    own_fore = own_back = own
    their_fore = their_back = theirs
    own_blocks, their_blocks = [own], [theirs]
    for _ in range(RING // 2 - 1):
        own_fore, own_back = shift(own_fore, "own", 1), shift(own_back, "own", -1)
        their_fore, their_back = shift(their_fore, "theirs", 1), shift(their_back, "theirs", -1)
        own_blocks += [own_fore, own_back]
        their_blocks += [their_fore, their_back]
    own_blocks.append(shift(own_fore, "own", 1))
    their_blocks.append(shift(their_fore, "theirs", 1))
    return own_blocks, their_blocks


DIMS = (((1,), (1,)), ((), ()))
LAST = RING - 1


def pad_kernel(*refs):
    out_ref = refs[3]
    for m in range(3):
        for e in range(E):
            out_ref[m, e, 16:PAD, :] = jnp.zeros((PAD - 16, D), jnp.bfloat16)
            out_ref[m, e, 0:HID, :] = refs[m][e]


def pad_rows(weights):
    return pl.pallas_call(
        pad_kernel,
        out_shape=jax.ShapeDtypeStruct((3, E, PAD, D), jnp.bfloat16),
        in_specs=[VMEM] * 3,
        out_specs=VMEM,
        compiler_params=pltpu.CompilerParams(vmem_limit_bytes=7 * MIB),
        cost_estimate=pl.CostEstimate(flops=0, bytes_accessed=9 * MIB, transcendentals=0),
    )(*weights)


def split_kernel(plane_ref, own_ref, their_ref):
    own_ref[...] = plane_ref[:, 0]
    their_ref[...] = plane_ref[:, 1]


def split(plane):
    half = jax.ShapeDtypeStruct((32, ROWS, FEATS), jnp.bfloat16)
    return pl.pallas_call(
        split_kernel,
        out_shape=(half, half),
        in_specs=[VMEM],
        out_specs=(VMEM, VMEM),
        compiler_params=pltpu.CompilerParams(vmem_limit_bytes=3 * MIB),
    )(plane)


def ring_place(mine, sign, offset):
    return lax.rem(mine + sign * offset + RING, RING)


def fill_tokens(tok_ref, blocks):
    for zl in range(2):
        for k in range(LAST):
            for t in range(16):
                tok_ref[zl, k * ROWS:(k + 1) * ROWS, t * FEATS:(t + 1) * FEATS] = blocks[k][zl * 16 + t]
        tok_ref[zl, LAST * ROWS:, :] = jnp.zeros((ROWS, D), jnp.bfloat16)


def fill_cotangents(cot_ref, blocks, my_z, sign, places):
    for j in range(LAST):
        z = ring_place(my_z, sign, OFFSETS[j])
        for x in range(4):
            for k in range(RING):
                cot_ref[z, k * ROWS:(k + 1) * ROWS, x * FEATS:(x + 1) * FEATS] = blocks[j][x * 8 + places[k]]
    cot_ref[ring_place(my_z, sign, OFFSETS[LAST])] = jnp.zeros((256, 4 * FEATS), jnp.bfloat16)


def weight_rows(mine_ref, other_ref, m):
    return jnp.concatenate([mine_ref[m], other_ref[m]], axis=0).reshape(2 * E * PAD, D)


def down_rows_of(mine_ref, other_ref, zh):
    lanes = [pl.ds(pl.multiple_of((x * 4 + zh) * FEATS, FEATS), FEATS) for x in range(4)]
    rows = [jnp.concatenate([ref[2, :, :, at] for at in lanes], axis=-1) for ref in (mine_ref, other_ref)]
    return jnp.concatenate(rows, axis=0).reshape(2 * E * PAD, 4 * FEATS)


def middle_kernel(place_ref, mine_ref, other_ref, *refs):
    own, theirs = refs[:LAST], refs[LAST:2 * LAST]
    acc_ref, tok_ref, cot_ref = refs[2 * LAST:]
    my_y, my_z, sign = place_ref[0], place_ref[1], place_ref[2]
    places = [ring_place(my_y, sign, OFFSETS[k]) for k in range(RING)]

    @pl.when(sign > 0)
    def _():
        fill_tokens(tok_ref, own)
        fill_cotangents(cot_ref, theirs, my_z, sign, places)

    @pl.when(sign < 0)
    def _():
        fill_tokens(tok_ref, theirs)
        fill_cotangents(cot_ref, own, my_z, sign, places)

    for m in range(2):
        rows = weight_rows(mine_ref, other_ref, m)
        for zl in range(2):
            got = lax.dot_general(rows, tok_ref[zl], DIMS, preferred_element_type=jnp.float32)
            acc_ref[m, zl] = got.reshape(2 * E, PAD, 256)
    for zl in range(2):
        total = None
        for zh in range(4):
            rows = down_rows_of(mine_ref, other_ref, zh)
            got = lax.dot_general(rows, cot_ref[zh * 2 + zl], DIMS, preferred_element_type=jnp.float32)
            total = got if total is None else total + got
        acc_ref[2, zl] = total.reshape(2 * E, PAD, 256)


def tail_kernel(place_ref, logits_ref, mine_ref, other_ref, acc_ref, own_ref, their_ref, out_ref, tok_ref, cot_ref, late_ref, back_ref):
    my_y, my_z, sign = place_ref[0], place_ref[1], place_ref[2]
    places = [ring_place(my_y, sign, OFFSETS[k]) for k in range(RING)]
    last_z = ring_place(my_z, sign, OFFSETS[LAST])

    def fill(a_ref, b_ref):
        for zl in range(2):
            for t in range(16):
                tok_ref[zl * 128 + 96:(zl + 1) * 128, t * FEATS:(t + 1) * FEATS] = a_ref[zl * 16 + t]
        for x in range(4):
            for k in range(RING):
                cot_ref[k * ROWS:(k + 1) * ROWS, x * FEATS:(x + 1) * FEATS] = b_ref[x * 8 + places[k]]

    for zl in range(2):
        tok_ref[zl * 128:zl * 128 + 96, :] = jnp.zeros((96, D), jnp.bfloat16)

    @pl.when(sign > 0)
    def _():
        fill(own_ref, their_ref)

    @pl.when(sign < 0)
    def _():
        fill(their_ref, own_ref)

    for m in range(2):
        rows = weight_rows(mine_ref, other_ref, m)
        got = lax.dot_general(rows, tok_ref[...], DIMS, preferred_element_type=jnp.float32)
        late_ref[m] = got.reshape(2 * E, PAD, 256)
    rows = down_rows_of(mine_ref, other_ref, last_z // 2)
    got = lax.dot_general(rows, cot_ref[...], DIMS, preferred_element_type=jnp.float32)
    back_ref[lax.rem(last_z, 2)] = got.reshape(2 * E, PAD, 256)
    back_ref[1 - lax.rem(last_z, 2)] = jnp.zeros((2 * E, PAD, 256), jnp.float32)

    lane = lax.broadcasted_iota(jnp.int32, (8, 128), 1)
    seg = lax.broadcasted_iota(jnp.int32, (8, 128), 0)
    belongs = []
    for half in range(2):
        lane_seg = jnp.zeros((8, 128), jnp.int32)
        for k in range(4):
            lane_seg = jnp.where(lane // ROWS == k, places[half * 4 + k], lane_seg)
        belongs.append(lane_seg == seg)
    mixing = softmax_rows(logits_ref[...])

    token_sums = []
    for half in range(2):
        lanes = slice(half * 128, (half + 1) * 128)
        mix = [
            jnp.sum(jnp.where(belongs[half], mixing[:, e:e + 1], 0.0), axis=0, keepdims=True) for e in range(E)
        ]
        sums = [jnp.zeros((8, 128), jnp.float32) for _ in range(E)]
        for zl in range(2):
            late = slice(zl * 128, (zl + 1) * 128)

            def add(i, sums, zl=zl, lanes=lanes, late=late, mix=mix, half=half):
                pair, rows = (i // 4) * E, pl.ds((i % 4) * 8, 8)
                gate = [acc_ref[0, zl, pair + e, rows, lanes] for e in range(E)]
                up = [acc_ref[1, zl, pair + e, rows, lanes] for e in range(E)]
                if half == 1:
                    gate = [g + late_ref[0, pair + e, rows, late] for e, g in enumerate(gate)]
                    up = [u + late_ref[1, pair + e, rows, late] for e, u in enumerate(up)]
                back = [acc_ref[2, zl, pair + e, rows, lanes] + back_ref[zl, pair + e, rows, lanes] for e in range(E)]
                gate_sum = sum(mix[e] * gate[e] for e in range(E))
                upward = sum(mix[e] * up[e] for e in range(E))
                backward = sum(mix[e] * back[e] for e in range(E))
                sigmoid = jax.nn.sigmoid(gate_sum)
                active = gate_sum * sigmoid
                hidden = active * upward
                grad_gate = backward * upward * sigmoid * (1.0 + gate_sum * (1.0 - sigmoid))
                grad_up = backward * active
                return [
                    sums[e] + (grad_gate * gate[e] + grad_up * up[e] + hidden * back[e]) for e in range(E)
                ]

            for i in range(8):
                sums = add(i, sums)
        token_sums.append([jnp.sum(sums[e], axis=0, keepdims=True) for e in range(E)])
    out = jnp.zeros((8, 128), jnp.float32)
    for e in range(E):
        picked = sum(jnp.where(belongs[half], token_sums[half][e], 0.0) for half in range(2))
        out = jnp.where(lane == e, jnp.sum(picked, axis=1, keepdims=True), out)
    out_ref[...] = jnp.broadcast_to(out[None], out_ref.shape)


def softmax_rows(logits):
    raised = jnp.exp(logits - jnp.max(logits, axis=-1, keepdims=True))
    return raised / jnp.sum(raised, axis=-1, keepdims=True)


def add_kernel(got_ref, out_ref):
    out_ref[...] = jnp.broadcast_to(jnp.sum(got_ref[...], axis=0)[None], out_ref.shape)


def finish_kernel(got_ref, logits_ref, merge_ref, router_ref):
    merge_grad = jnp.sum(got_ref[...], axis=0)[:, :E]
    mixing = softmax_rows(logits_ref[...])
    merge_ref[...] = merge_grad
    router_ref[...] = mixing * (
        merge_grad - jnp.sum(mixing * merge_grad, axis=-1, keepdims=True)
    )


def on_device(tokens, cotangent, gate_rows, up_rows, down_rows, router_logits):
    my_y = lax.axis_index("y")
    my_z = lax.axis_index("zh") * 2 + lax.axis_index("zl")
    core = lax.axis_index("c")
    sign = 1 - 2 * core
    place = jnp.stack([my_y, my_z, sign]).astype(jnp.int32)
    place, *mine = lax.optimization_barrier((place, gate_rows, up_rows, down_rows))
    keep = jnp.where(core == 0, tokens, cotangent)
    got = swap_cores(jnp.where(core == 0, cotangent, tokens))
    pair = jnp.stack([keep, got])
    plane = lax.all_to_all(
        jnp.broadcast_to(pair[None], (32,) + pair.shape), ALL, 0, 0, axis_index_groups=plane_groups()
    )
    other = [swap_cores(w) for w in mine]
    mine, other = pad_rows(mine), pad_rows(other)
    plane, mine, other = lax.optimization_barrier((plane, mine, other))
    own, give = split(plane)
    own_blocks, their_blocks = rings(own, swap_cores(give))

    acc_shape = (3, 2, 2 * E, PAD, 256)
    acc = pl.pallas_call(
        middle_kernel,
        out_shape=jax.ShapeDtypeStruct(acc_shape, jnp.float32),
        in_specs=[SMEM] + [VMEM] * (2 + 2 * LAST),
        out_specs=VMEM,
        scratch_shapes=[
            pltpu.VMEM((2, 256, D), jnp.bfloat16),
            pltpu.VMEM((8, 256, 4 * FEATS), jnp.bfloat16),
        ],
        compiler_params=pltpu.CompilerParams(vmem_limit_bytes=14 * MIB),
        cost_estimate=pl.CostEstimate(flops=9_000_000_000, bytes_accessed=24 * MIB, transcendentals=0),
    )(place, mine, other, *own_blocks[:LAST], *their_blocks[:LAST])
    part = pl.pallas_call(
        tail_kernel,
        out_shape=jax.ShapeDtypeStruct((32, 8, 128), jnp.float32),
        in_specs=[SMEM] + [VMEM] * 6,
        out_specs=VMEM,
        scratch_shapes=[
            pltpu.VMEM((256, D), jnp.bfloat16),
            pltpu.VMEM((256, 4 * FEATS), jnp.bfloat16),
            pltpu.VMEM((2, 2 * E, PAD, 256), jnp.float32),
            pltpu.VMEM((2, 2 * E, PAD, 256), jnp.float32),
        ],
        compiler_params=pltpu.CompilerParams(vmem_limit_bytes=8 * MIB),
    )(place, router_logits, mine, other, acc, own_blocks[LAST], their_blocks[LAST])
    got = lax.all_to_all(part, ("x", "y"), 0, 0)
    part = pl.pallas_call(
        add_kernel,
        out_shape=jax.ShapeDtypeStruct((16, 8, 128), jnp.float32),
        in_specs=[VMEM],
        out_specs=VMEM,
        compiler_params=pltpu.CompilerParams(vmem_limit_bytes=2 * MIB),
    )(got)
    got = lax.all_to_all(part, ("zl", "zh", "c"), 0, 0)
    small = jax.ShapeDtypeStruct((8, E), jnp.float32)
    return pl.pallas_call(
        finish_kernel,
        out_shape=(small, small),
        in_specs=[VMEM, VMEM],
        out_specs=(VMEM, VMEM),
        compiler_params=pltpu.CompilerParams(vmem_limit_bytes=2 * MIB),
    )(got, router_logits)


def solution(mesh):
    fine = Mesh(mesh.devices.reshape(8, 2, 2, 4, 4), ("y", "zl", "c", "x", "zh"))
    dp, tensor = ("y", "zl", "c"), ("x", "zh")
    weights = P(None, dp + tensor, None)
    return jax.shard_map(
        on_device,
        mesh=fine,
        in_specs=(P(dp, tensor), P(dp, tensor), weights, weights, weights, P()),
        out_specs=(P(), P()),
        check_vma=False,
    )
```

```python
import itertools

import jax
import jax.numpy as jnp
from jax import lax
from jax.experimental import pallas as pl
from jax.experimental.pallas import tpu as pltpu
from jax.sharding import Mesh, PartitionSpec as P

E = 6
HID = 28
PAD = 32
D = 4096
ROWS = 32
FEATS = 256
RING = 8
MIB = 1024 * 1024
VMEM = pl.BlockSpec(memory_space=pltpu.VMEM)
SMEM = pl.BlockSpec(memory_space=pltpu.SMEM)
HBM = pl.BlockSpec(memory_space=pltpu.HBM)
ALL = ("y", "zl", "c", "x", "zh")
OFFSETS = (0, -1, 1, -2, 2, -3, 3, 4)


def device(y, z, core, x):
    y, z = y % 8, z % 8
    return (((y * 2 + z % 2) * 2 + core) * 4 + x) * 4 + z // 2


PLACES = tuple(itertools.product(range(8), range(8), range(2), range(4)))


def shift(block, whose, step):
    pairs = []
    for y, z, core, x in PLACES:
        go = step if core == 0 else -step
        along_y = (core == 0) == (whose == "own")
        to = (y + go, z, core, x) if along_y else (y, z + go, core, x)
        pairs.append((device(y, z, core, x), device(*to)))
    return lax.ppermute(block, ALL, pairs)


def swap_cores(block):
    return lax.ppermute(block, "c", [(0, 1), (1, 0)])


def plane_groups():
    first = [
        [device(y, zl + 2 * zh, 0, x) for zl in range(2) for x in range(4) for zh in range(4)]
        for y in range(8)
    ]
    second = [[device(y, z, 1, x) for x in range(4) for y in range(8)] for z in range(8)]
    return first + second


def rings(own, theirs):
    own_fore = own_back = own
    their_fore = their_back = theirs
    own_blocks, their_blocks = [own], [theirs]
    for _ in range(RING // 2 - 1):
        own_fore, own_back = shift(own_fore, "own", 1), shift(own_back, "own", -1)
        their_fore, their_back = shift(their_fore, "theirs", 1), shift(their_back, "theirs", -1)
        own_blocks += [own_fore, own_back]
        their_blocks += [their_fore, their_back]
    own_blocks.append(shift(own_fore, "own", 1))
    their_blocks.append(shift(their_fore, "theirs", 1))
    return own_blocks, their_blocks


DIMS = (((1,), (1,)), ((), ()))
LAST = RING - 1


def pad_kernel(*refs):
    out_ref, done_ref = refs[3:]
    done_ref[...] = jnp.zeros(done_ref.shape, jnp.float32)
    for m in range(3):
        for e in range(E):
            out_ref[m, e, 16:PAD, :] = jnp.zeros((PAD - 16, D), jnp.bfloat16)
            out_ref[m, e, 0:HID, :] = refs[m][e]


def pad_rows(weights):
    return pl.pallas_call(
        pad_kernel,
        out_shape=(jax.ShapeDtypeStruct((3, E, PAD, D), jnp.bfloat16), jax.ShapeDtypeStruct((8, 128), jnp.float32)),
        in_specs=[VMEM] * 3,
        out_specs=(VMEM, VMEM),
        compiler_params=pltpu.CompilerParams(vmem_limit_bytes=7 * MIB),
        cost_estimate=pl.CostEstimate(flops=0, bytes_accessed=9 * MIB, transcendentals=0),
    )(*weights)


def split_kernel(plane_ref, mine_done_ref, other_done_ref, own_ref, their_ref):
    own_ref[...] = plane_ref[:, 0]
    their_ref[...] = plane_ref[:, 1]


def split(plane, *done):
    half = jax.ShapeDtypeStruct((32, ROWS, FEATS), jnp.bfloat16)
    return pl.pallas_call(
        split_kernel,
        out_shape=(half, half),
        in_specs=[VMEM] * 3,
        out_specs=(VMEM, VMEM),
        compiler_params=pltpu.CompilerParams(vmem_limit_bytes=3 * MIB),
    )(plane, *done)


def ring_place(mine, sign, offset):
    return lax.rem(mine + sign * offset + RING, RING)


def fill_tokens(tok_ref, blocks):
    for zl in range(2):
        for k in range(LAST):
            for t in range(16):
                tok_ref[zl, k * ROWS:(k + 1) * ROWS, t * FEATS:(t + 1) * FEATS] = blocks[k][zl * 16 + t]
        tok_ref[zl, LAST * ROWS:, :] = jnp.zeros((ROWS, D), jnp.bfloat16)


def fill_cotangents(cot_ref, blocks, my_z, sign, places):
    for j in range(LAST):
        z = ring_place(my_z, sign, OFFSETS[j])
        for x in range(4):
            for k in range(RING):
                cot_ref[z, k * ROWS:(k + 1) * ROWS, x * FEATS:(x + 1) * FEATS] = blocks[j][x * 8 + places[k]]
    cot_ref[ring_place(my_z, sign, OFFSETS[LAST])] = jnp.zeros((256, 4 * FEATS), jnp.bfloat16)


def weight_rows(w_ref, m):
    return w_ref[m].reshape(2 * E * PAD, D)


def down_rows_of(w_ref, zh):
    lanes = [pl.ds(pl.multiple_of((x * 4 + zh) * FEATS, FEATS), FEATS) for x in range(4)]
    return jnp.concatenate([w_ref[2, :, :, :, at] for at in lanes], axis=-1).reshape(2 * E * PAD, 4 * FEATS)


def middle_kernel(place_ref, mine_ref, other_ref, *refs):
    own, theirs = refs[:LAST], refs[LAST:2 * LAST]
    acc_ref, w_ref, tok_ref, cot_ref, sems = refs[2 * LAST:]
    my_y, my_z, sign = place_ref[0], place_ref[1], place_ref[2]
    copies = [
        [
            pltpu.make_async_copy(source.at[m], w_ref.at[m, p], sems.at[m, p])
            for p, source in enumerate((mine_ref, other_ref))
        ]
        for m in range(3)
    ]
    for pair in copies:
        for copy in pair:
            copy.start()
    places = [ring_place(my_y, sign, OFFSETS[k]) for k in range(RING)]

    @pl.when(sign > 0)
    def _():
        fill_tokens(tok_ref, own)
        fill_cotangents(cot_ref, theirs, my_z, sign, places)

    @pl.when(sign < 0)
    def _():
        fill_tokens(tok_ref, theirs)
        fill_cotangents(cot_ref, own, my_z, sign, places)

    for m in range(2):
        for copy in copies[m]:
            copy.wait()
        rows = weight_rows(w_ref, m)
        for zl in range(2):
            got = lax.dot_general(rows, tok_ref[zl], DIMS, preferred_element_type=jnp.float32)
            acc_ref[m, zl] = got.reshape(2 * E, PAD, 256)
    for copy in copies[2]:
        copy.wait()
    for zl in range(2):
        total = None
        for zh in range(4):
            rows = down_rows_of(w_ref, zh)
            got = lax.dot_general(rows, cot_ref[zh * 2 + zl], DIMS, preferred_element_type=jnp.float32)
            total = got if total is None else total + got
        acc_ref[2, zl] = total.reshape(2 * E, PAD, 256)


def tail_kernel(place_ref, logits_ref, w_ref, acc_ref, own_ref, their_ref, out_ref, tok_ref, cot_ref, late_ref, back_ref):
    my_y, my_z, sign = place_ref[0], place_ref[1], place_ref[2]
    places = [ring_place(my_y, sign, OFFSETS[k]) for k in range(RING)]
    last_z = ring_place(my_z, sign, OFFSETS[LAST])

    def fill(a_ref, b_ref):
        for zl in range(2):
            for t in range(16):
                tok_ref[zl * 128 + 96:(zl + 1) * 128, t * FEATS:(t + 1) * FEATS] = a_ref[zl * 16 + t]
        for x in range(4):
            for k in range(RING):
                cot_ref[k * ROWS:(k + 1) * ROWS, x * FEATS:(x + 1) * FEATS] = b_ref[x * 8 + places[k]]

    for zl in range(2):
        tok_ref[zl * 128:zl * 128 + 96, :] = jnp.zeros((96, D), jnp.bfloat16)

    @pl.when(sign > 0)
    def _():
        fill(own_ref, their_ref)

    @pl.when(sign < 0)
    def _():
        fill(their_ref, own_ref)

    for m in range(2):
        rows = weight_rows(w_ref, m)
        got = lax.dot_general(rows, tok_ref[...], DIMS, preferred_element_type=jnp.float32)
        late_ref[m] = got.reshape(2 * E, PAD, 256)
    rows = down_rows_of(w_ref, last_z // 2)
    got = lax.dot_general(rows, cot_ref[...], DIMS, preferred_element_type=jnp.float32)
    back_ref[lax.rem(last_z, 2)] = got.reshape(2 * E, PAD, 256)
    back_ref[1 - lax.rem(last_z, 2)] = jnp.zeros((2 * E, PAD, 256), jnp.float32)

    lane = lax.broadcasted_iota(jnp.int32, (8, 128), 1)
    seg = lax.broadcasted_iota(jnp.int32, (8, 128), 0)
    belongs = []
    for half in range(2):
        lane_seg = jnp.zeros((8, 128), jnp.int32)
        for k in range(4):
            lane_seg = jnp.where(lane // ROWS == k, places[half * 4 + k], lane_seg)
        belongs.append(lane_seg == seg)
    mixing = softmax_rows(logits_ref[...])

    token_sums = []
    for half in range(2):
        lanes = slice(half * 128, (half + 1) * 128)
        mix = [
            jnp.sum(jnp.where(belongs[half], mixing[:, e:e + 1], 0.0), axis=0, keepdims=True) for e in range(E)
        ]
        sums = [jnp.zeros((8, 128), jnp.float32) for _ in range(E)]
        for zl in range(2):
            late = slice(zl * 128, (zl + 1) * 128)

            def add(i, sums, zl=zl, lanes=lanes, late=late, mix=mix, half=half):
                pair, rows = (i // 4) * E, pl.ds((i % 4) * 8, 8)
                gate = [acc_ref[0, zl, pair + e, rows, lanes] for e in range(E)]
                up = [acc_ref[1, zl, pair + e, rows, lanes] for e in range(E)]
                if half == 1:
                    gate = [g + late_ref[0, pair + e, rows, late] for e, g in enumerate(gate)]
                    up = [u + late_ref[1, pair + e, rows, late] for e, u in enumerate(up)]
                back = [acc_ref[2, zl, pair + e, rows, lanes] + back_ref[zl, pair + e, rows, lanes] for e in range(E)]
                gate_sum = sum(mix[e] * gate[e] for e in range(E))
                upward = sum(mix[e] * up[e] for e in range(E))
                backward = sum(mix[e] * back[e] for e in range(E))
                sigmoid = jax.nn.sigmoid(gate_sum)
                active = gate_sum * sigmoid
                hidden = active * upward
                grad_gate = backward * upward * sigmoid * (1.0 + gate_sum * (1.0 - sigmoid))
                grad_up = backward * active
                return [
                    sums[e] + (grad_gate * gate[e] + grad_up * up[e] + hidden * back[e]) for e in range(E)
                ]

            for i in range(8):
                sums = add(i, sums)
        token_sums.append([jnp.sum(sums[e], axis=0, keepdims=True) for e in range(E)])
    out = jnp.zeros((8, 128), jnp.float32)
    for e in range(E):
        picked = sum(jnp.where(belongs[half], token_sums[half][e], 0.0) for half in range(2))
        out = jnp.where(lane == e, jnp.sum(picked, axis=1, keepdims=True), out)
    out_ref[...] = jnp.broadcast_to(out[None], out_ref.shape)


def softmax_rows(logits):
    raised = jnp.exp(logits - jnp.max(logits, axis=-1, keepdims=True))
    return raised / jnp.sum(raised, axis=-1, keepdims=True)


def add_kernel(got_ref, out_ref):
    out_ref[...] = jnp.broadcast_to(jnp.sum(got_ref[...], axis=0)[None], out_ref.shape)


def finish_kernel(got_ref, logits_ref, merge_ref, router_ref):
    merge_grad = jnp.sum(got_ref[...], axis=0)[:, :E]
    mixing = softmax_rows(logits_ref[...])
    merge_ref[...] = merge_grad
    router_ref[...] = mixing * (
        merge_grad - jnp.sum(mixing * merge_grad, axis=-1, keepdims=True)
    )


def on_device(tokens, cotangent, gate_rows, up_rows, down_rows, router_logits):
    my_y = lax.axis_index("y")
    my_z = lax.axis_index("zh") * 2 + lax.axis_index("zl")
    core = lax.axis_index("c")
    sign = 1 - 2 * core
    place = jnp.stack([my_y, my_z, sign]).astype(jnp.int32)
    place, *mine = lax.optimization_barrier((place, gate_rows, up_rows, down_rows))
    keep = jnp.where(core == 0, tokens, cotangent)
    got = swap_cores(jnp.where(core == 0, cotangent, tokens))
    pair = jnp.stack([keep, got])
    plane = lax.all_to_all(
        jnp.broadcast_to(pair[None], (32,) + pair.shape), ALL, 0, 0, axis_index_groups=plane_groups()
    )
    other = [swap_cores(w) for w in mine]
    (mine, mine_done), (other, other_done) = pad_rows(mine), pad_rows(other)
    own, give = split(plane, mine_done, other_done)
    own_blocks, their_blocks = rings(own, swap_cores(give))

    acc_shape = (3, 2, 2 * E, PAD, 256)
    mine, other = (pltpu.with_memory_space_constraint(w, pltpu.HBM) for w in (mine, other))
    acc, weights = pl.pallas_call(
        middle_kernel,
        out_shape=(
            jax.ShapeDtypeStruct(acc_shape, jnp.float32),
            pltpu.VMEM((3, 2, E, PAD, D), jnp.bfloat16),
        ),
        in_specs=[SMEM, HBM, HBM] + [VMEM] * (2 * LAST),
        out_specs=(VMEM, VMEM),
        scratch_shapes=[
            pltpu.VMEM((2, 256, D), jnp.bfloat16),
            pltpu.VMEM((8, 256, 4 * FEATS), jnp.bfloat16),
            pltpu.SemaphoreType.DMA((3, 2)),
        ],
        compiler_params=pltpu.CompilerParams(vmem_limit_bytes=14 * MIB),
        cost_estimate=pl.CostEstimate(flops=9_000_000_000, bytes_accessed=24 * MIB, transcendentals=0),
    )(place, mine, other, *own_blocks[:LAST], *their_blocks[:LAST])
    part = pl.pallas_call(
        tail_kernel,
        out_shape=jax.ShapeDtypeStruct((32, 8, 128), jnp.float32),
        in_specs=[SMEM] + [VMEM] * 5,
        out_specs=VMEM,
        scratch_shapes=[
            pltpu.VMEM((256, D), jnp.bfloat16),
            pltpu.VMEM((256, 4 * FEATS), jnp.bfloat16),
            pltpu.VMEM((2, 2 * E, PAD, 256), jnp.float32),
            pltpu.VMEM((2, 2 * E, PAD, 256), jnp.float32),
        ],
        compiler_params=pltpu.CompilerParams(vmem_limit_bytes=8 * MIB),
    )(place, router_logits, weights, acc, own_blocks[LAST], their_blocks[LAST])
    got = lax.all_to_all(part, ("x", "y"), 0, 0)
    part = pl.pallas_call(
        add_kernel,
        out_shape=jax.ShapeDtypeStruct((16, 8, 128), jnp.float32),
        in_specs=[VMEM],
        out_specs=VMEM,
        compiler_params=pltpu.CompilerParams(vmem_limit_bytes=2 * MIB),
    )(got)
    got = lax.all_to_all(part, ("zl", "zh", "c"), 0, 0)
    small = jax.ShapeDtypeStruct((8, E), jnp.float32)
    return pl.pallas_call(
        finish_kernel,
        out_shape=(small, small),
        in_specs=[VMEM, VMEM],
        out_specs=(VMEM, VMEM),
        compiler_params=pltpu.CompilerParams(vmem_limit_bytes=2 * MIB),
    )(got, router_logits)


def solution(mesh):
    fine = Mesh(mesh.devices.reshape(8, 2, 2, 4, 4), ("y", "zl", "c", "x", "zh"))
    dp, tensor = ("y", "zl", "c"), ("x", "zh")
    weights = P(None, dp + tensor, None)
    return jax.shard_map(
        on_device,
        mesh=fine,
        in_specs=(P(dp, tensor), P(dp, tensor), weights, weights, weights, P()),
        out_specs=(P(), P()),
        check_vma=False,
    )
```

```python
import itertools

import jax
import jax.numpy as jnp
from jax import lax
from jax.experimental import pallas as pl
from jax.experimental.pallas import tpu as pltpu
from jax.sharding import Mesh, PartitionSpec as P

E = 6
HID = 28
PAD = 32
D = 4096
ROWS = 32
FEATS = 256
RING = 8
MIB = 1024 * 1024
VMEM = pl.BlockSpec(memory_space=pltpu.VMEM)
SMEM = pl.BlockSpec(memory_space=pltpu.SMEM)
HBM = pl.BlockSpec(memory_space=pltpu.HBM)
ALL = ("y", "zl", "c", "x", "zh")
OFFSETS = (0, -1, 1, -2, 2, -3, 3, 4)


def device(y, z, core, x):
    y, z = y % 8, z % 8
    return (((y * 2 + z % 2) * 2 + core) * 4 + x) * 4 + z // 2


PLACES = tuple(itertools.product(range(8), range(8), range(2), range(4)))


def shift(block, whose, step):
    pairs = []
    for y, z, core, x in PLACES:
        go = step if core == 0 else -step
        along_y = (core == 0) == (whose == "own")
        to = (y + go, z, core, x) if along_y else (y, z + go, core, x)
        pairs.append((device(y, z, core, x), device(*to)))
    return lax.ppermute(block, ALL, pairs)


def swap_cores(block):
    return lax.ppermute(block, "c", [(0, 1), (1, 0)])


def plane_groups():
    first = [
        [device(y, zl + 2 * zh, 0, x) for zl in range(2) for x in range(4) for zh in range(4)]
        for y in range(8)
    ]
    second = [[device(y, z, 1, x) for x in range(4) for y in range(8)] for z in range(8)]
    return first + second


def rings(own, theirs):
    own_fore = own_back = own
    their_fore = their_back = theirs
    own_blocks, their_blocks = [own], [theirs]
    for _ in range(RING // 2 - 1):
        own_fore, own_back = shift(own_fore, "own", 1), shift(own_back, "own", -1)
        their_back, their_fore = shift(their_back, "theirs", -1), shift(their_fore, "theirs", 1)
        own_fore, own_back = lax.optimization_barrier((own_fore, own_back))
        their_back, their_fore = lax.optimization_barrier((their_back, their_fore))
        own_blocks += [own_fore, own_back]
        their_blocks += [their_fore, their_back]
    own_blocks.append(shift(own_fore, "own", 1))
    their_blocks.append(shift(their_fore, "theirs", 1))
    return own_blocks, their_blocks


DIMS = (((1,), (1,)), ((), ()))
LAST = RING - 1


def pad_kernel(*refs):
    out_ref, done_ref = refs[3:]
    done_ref[...] = jnp.zeros(done_ref.shape, jnp.float32)
    for m in range(3):
        for e in range(E):
            out_ref[m, e, 16:PAD, :] = jnp.zeros((PAD - 16, D), jnp.bfloat16)
            out_ref[m, e, 0:HID, :] = refs[m][e]


def pad_rows(weights):
    return pl.pallas_call(
        pad_kernel,
        out_shape=(jax.ShapeDtypeStruct((3, E, PAD, D), jnp.bfloat16), jax.ShapeDtypeStruct((8, 128), jnp.float32)),
        in_specs=[VMEM] * 3,
        out_specs=(VMEM, VMEM),
        compiler_params=pltpu.CompilerParams(vmem_limit_bytes=7 * MIB),
        cost_estimate=pl.CostEstimate(flops=0, bytes_accessed=9 * MIB, transcendentals=0),
    )(*weights)


def split_kernel(plane_ref, mine_done_ref, other_done_ref, own_ref, their_ref):
    own_ref[...] = plane_ref[:, 0]
    their_ref[...] = plane_ref[:, 1]


def split(plane, *done):
    half = jax.ShapeDtypeStruct((32, ROWS, FEATS), jnp.bfloat16)
    return pl.pallas_call(
        split_kernel,
        out_shape=(half, half),
        in_specs=[VMEM] * 3,
        out_specs=(VMEM, VMEM),
        compiler_params=pltpu.CompilerParams(vmem_limit_bytes=3 * MIB),
    )(plane, *done)


def ring_place(mine, sign, offset):
    return lax.rem(mine + sign * offset + RING, RING)


def fill_tokens(tok_ref, blocks):
    for zl in range(2):
        for k in range(LAST):
            for t in range(16):
                tok_ref[zl, k * ROWS:(k + 1) * ROWS, t * FEATS:(t + 1) * FEATS] = blocks[k][zl * 16 + t]
        tok_ref[zl, LAST * ROWS:, :] = jnp.zeros((ROWS, D), jnp.bfloat16)


def fill_cotangents(cot_ref, blocks, my_z, sign, places):
    for j in range(LAST):
        z = ring_place(my_z, sign, OFFSETS[j])
        for x in range(4):
            for k in range(RING):
                cot_ref[z, k * ROWS:(k + 1) * ROWS, x * FEATS:(x + 1) * FEATS] = blocks[j][x * 8 + places[k]]
    cot_ref[ring_place(my_z, sign, OFFSETS[LAST])] = jnp.zeros((256, 4 * FEATS), jnp.bfloat16)


def weight_rows(w_ref, m):
    return w_ref[m].reshape(2 * E * PAD, D)


def down_rows_of(w_ref, zh):
    lanes = [pl.ds(pl.multiple_of((x * 4 + zh) * FEATS, FEATS), FEATS) for x in range(4)]
    return jnp.concatenate([w_ref[2, :, :, :, at] for at in lanes], axis=-1).reshape(2 * E * PAD, 4 * FEATS)


def middle_kernel(place_ref, mine_ref, other_ref, *refs):
    own, theirs = refs[:LAST], refs[LAST:2 * LAST]
    acc_ref, w_ref, tok_ref, cot_ref, sems = refs[2 * LAST:]
    my_y, my_z, sign = place_ref[0], place_ref[1], place_ref[2]
    copies = [
        [
            pltpu.make_async_copy(source.at[m], w_ref.at[m, p], sems.at[m, p])
            for p, source in enumerate((mine_ref, other_ref))
        ]
        for m in range(3)
    ]
    for pair in copies:
        for copy in pair:
            copy.start()
    places = [ring_place(my_y, sign, OFFSETS[k]) for k in range(RING)]

    @pl.when(sign > 0)
    def _():
        fill_tokens(tok_ref, own)
        fill_cotangents(cot_ref, theirs, my_z, sign, places)

    @pl.when(sign < 0)
    def _():
        fill_tokens(tok_ref, theirs)
        fill_cotangents(cot_ref, own, my_z, sign, places)

    for m in range(2):
        for copy in copies[m]:
            copy.wait()
        rows = weight_rows(w_ref, m)
        for zl in range(2):
            got = lax.dot_general(rows, tok_ref[zl], DIMS, preferred_element_type=jnp.float32)
            acc_ref[m, zl] = got.reshape(2 * E, PAD, 256)
    for copy in copies[2]:
        copy.wait()
    for zl in range(2):
        total = None
        for zh in range(4):
            rows = down_rows_of(w_ref, zh)
            got = lax.dot_general(rows, cot_ref[zh * 2 + zl], DIMS, preferred_element_type=jnp.float32)
            total = got if total is None else total + got
        acc_ref[2, zl] = total.reshape(2 * E, PAD, 256)


def tail_kernel(place_ref, logits_ref, w_ref, acc_ref, own_ref, their_ref, out_ref, tok_ref, cot_ref, late_ref, back_ref):
    my_y, my_z, sign = place_ref[0], place_ref[1], place_ref[2]
    places = [ring_place(my_y, sign, OFFSETS[k]) for k in range(RING)]
    last_z = ring_place(my_z, sign, OFFSETS[LAST])

    def fill(a_ref, b_ref):
        for zl in range(2):
            for t in range(16):
                tok_ref[zl * 128 + 96:(zl + 1) * 128, t * FEATS:(t + 1) * FEATS] = a_ref[zl * 16 + t]
        for x in range(4):
            for k in range(RING):
                cot_ref[k * ROWS:(k + 1) * ROWS, x * FEATS:(x + 1) * FEATS] = b_ref[x * 8 + places[k]]

    for zl in range(2):
        tok_ref[zl * 128:zl * 128 + 96, :] = jnp.zeros((96, D), jnp.bfloat16)

    @pl.when(sign > 0)
    def _():
        fill(own_ref, their_ref)

    @pl.when(sign < 0)
    def _():
        fill(their_ref, own_ref)

    for m in range(2):
        rows = weight_rows(w_ref, m)
        got = lax.dot_general(rows, tok_ref[...], DIMS, preferred_element_type=jnp.float32)
        late_ref[m] = got.reshape(2 * E, PAD, 256)
    rows = down_rows_of(w_ref, last_z // 2)
    got = lax.dot_general(rows, cot_ref[...], DIMS, preferred_element_type=jnp.float32)
    back_ref[lax.rem(last_z, 2)] = got.reshape(2 * E, PAD, 256)
    back_ref[1 - lax.rem(last_z, 2)] = jnp.zeros((2 * E, PAD, 256), jnp.float32)

    lane = lax.broadcasted_iota(jnp.int32, (8, 128), 1)
    seg = lax.broadcasted_iota(jnp.int32, (8, 128), 0)
    belongs = []
    for half in range(2):
        lane_seg = jnp.zeros((8, 128), jnp.int32)
        for k in range(4):
            lane_seg = jnp.where(lane // ROWS == k, places[half * 4 + k], lane_seg)
        belongs.append(lane_seg == seg)
    mixing = softmax_rows(logits_ref[...])

    token_sums = []
    for half in range(2):
        lanes = slice(half * 128, (half + 1) * 128)
        mix = [
            jnp.sum(jnp.where(belongs[half], mixing[:, e:e + 1], 0.0), axis=0, keepdims=True) for e in range(E)
        ]
        sums = [jnp.zeros((8, 128), jnp.float32) for _ in range(E)]
        for zl in range(2):
            late = slice(zl * 128, (zl + 1) * 128)

            def add(i, sums, zl=zl, lanes=lanes, late=late, mix=mix, half=half):
                pair, rows = (i // 4) * E, pl.ds((i % 4) * 8, 8)
                gate = [acc_ref[0, zl, pair + e, rows, lanes] for e in range(E)]
                up = [acc_ref[1, zl, pair + e, rows, lanes] for e in range(E)]
                if half == 1:
                    gate = [g + late_ref[0, pair + e, rows, late] for e, g in enumerate(gate)]
                    up = [u + late_ref[1, pair + e, rows, late] for e, u in enumerate(up)]
                back = [acc_ref[2, zl, pair + e, rows, lanes] + back_ref[zl, pair + e, rows, lanes] for e in range(E)]
                gate_sum = sum(mix[e] * gate[e] for e in range(E))
                upward = sum(mix[e] * up[e] for e in range(E))
                backward = sum(mix[e] * back[e] for e in range(E))
                sigmoid = jax.nn.sigmoid(gate_sum)
                active = gate_sum * sigmoid
                hidden = active * upward
                grad_gate = backward * upward * sigmoid * (1.0 + gate_sum * (1.0 - sigmoid))
                grad_up = backward * active
                return [
                    sums[e] + (grad_gate * gate[e] + grad_up * up[e] + hidden * back[e]) for e in range(E)
                ]

            for i in range(8):
                sums = add(i, sums)
        token_sums.append([jnp.sum(sums[e], axis=0, keepdims=True) for e in range(E)])
    out = jnp.zeros((8, 128), jnp.float32)
    for e in range(E):
        picked = sum(jnp.where(belongs[half], token_sums[half][e], 0.0) for half in range(2))
        out = jnp.where(lane == e, jnp.sum(picked, axis=1, keepdims=True), out)
    out_ref[...] = jnp.broadcast_to(out[None], out_ref.shape)


def softmax_rows(logits):
    raised = jnp.exp(logits - jnp.max(logits, axis=-1, keepdims=True))
    return raised / jnp.sum(raised, axis=-1, keepdims=True)


def add_kernel(got_ref, out_ref):
    out_ref[...] = jnp.broadcast_to(jnp.sum(got_ref[...], axis=0)[None], out_ref.shape)


def finish_kernel(got_ref, logits_ref, merge_ref, router_ref):
    merge_grad = jnp.sum(got_ref[...], axis=0)[:, :E]
    mixing = softmax_rows(logits_ref[...])
    merge_ref[...] = merge_grad
    router_ref[...] = mixing * (
        merge_grad - jnp.sum(mixing * merge_grad, axis=-1, keepdims=True)
    )


def on_device(tokens, cotangent, gate_rows, up_rows, down_rows, router_logits):
    my_y = lax.axis_index("y")
    my_z = lax.axis_index("zh") * 2 + lax.axis_index("zl")
    core = lax.axis_index("c")
    sign = 1 - 2 * core
    place = jnp.stack([my_y, my_z, sign]).astype(jnp.int32)
    place, *mine = lax.optimization_barrier((place, gate_rows, up_rows, down_rows))
    keep = jnp.where(core == 0, tokens, cotangent)
    got = swap_cores(jnp.where(core == 0, cotangent, tokens))
    pair = jnp.stack([keep, got])
    plane = lax.all_to_all(
        jnp.broadcast_to(pair[None], (32,) + pair.shape), ALL, 0, 0, axis_index_groups=plane_groups()
    )
    other = [swap_cores(w) for w in mine]
    (mine, mine_done), (other, other_done) = pad_rows(mine), pad_rows(other)
    own, give = split(plane, mine_done, other_done)
    own_blocks, their_blocks = rings(own, swap_cores(give))

    acc_shape = (3, 2, 2 * E, PAD, 256)
    mine, other = (pltpu.with_memory_space_constraint(w, pltpu.HBM) for w in (mine, other))
    acc, weights = pl.pallas_call(
        middle_kernel,
        out_shape=(
            jax.ShapeDtypeStruct(acc_shape, jnp.float32),
            pltpu.VMEM((3, 2, E, PAD, D), jnp.bfloat16),
        ),
        in_specs=[SMEM, HBM, HBM] + [VMEM] * (2 * LAST),
        out_specs=(VMEM, VMEM),
        scratch_shapes=[
            pltpu.VMEM((2, 256, D), jnp.bfloat16),
            pltpu.VMEM((8, 256, 4 * FEATS), jnp.bfloat16),
            pltpu.SemaphoreType.DMA((3, 2)),
        ],
        compiler_params=pltpu.CompilerParams(vmem_limit_bytes=14 * MIB),
        cost_estimate=pl.CostEstimate(flops=9_000_000_000, bytes_accessed=24 * MIB, transcendentals=0),
    )(place, mine, other, *own_blocks[:LAST], *their_blocks[:LAST])
    part = pl.pallas_call(
        tail_kernel,
        out_shape=jax.ShapeDtypeStruct((32, 8, 128), jnp.float32),
        in_specs=[SMEM] + [VMEM] * 5,
        out_specs=VMEM,
        scratch_shapes=[
            pltpu.VMEM((256, D), jnp.bfloat16),
            pltpu.VMEM((256, 4 * FEATS), jnp.bfloat16),
            pltpu.VMEM((2, 2 * E, PAD, 256), jnp.float32),
            pltpu.VMEM((2, 2 * E, PAD, 256), jnp.float32),
        ],
        compiler_params=pltpu.CompilerParams(vmem_limit_bytes=8 * MIB),
    )(place, router_logits, weights, acc, own_blocks[LAST], their_blocks[LAST])
    got = lax.all_to_all(part, ("x", "y"), 0, 0)
    part = pl.pallas_call(
        add_kernel,
        out_shape=jax.ShapeDtypeStruct((16, 8, 128), jnp.float32),
        in_specs=[VMEM],
        out_specs=VMEM,
        compiler_params=pltpu.CompilerParams(vmem_limit_bytes=2 * MIB),
    )(got)
    got = lax.all_to_all(part, ("zl", "zh", "c"), 0, 0)
    small = jax.ShapeDtypeStruct((8, E), jnp.float32)
    return pl.pallas_call(
        finish_kernel,
        out_shape=(small, small),
        in_specs=[VMEM, VMEM],
        out_specs=(VMEM, VMEM),
        compiler_params=pltpu.CompilerParams(vmem_limit_bytes=2 * MIB),
    )(got, router_logits)


def solution(mesh):
    fine = Mesh(mesh.devices.reshape(8, 2, 2, 4, 4), ("y", "zl", "c", "x", "zh"))
    dp, tensor = ("y", "zl", "c"), ("x", "zh")
    weights = P(None, dp + tensor, None)
    return jax.shard_map(
        on_device,
        mesh=fine,
        in_specs=(P(dp, tensor), P(dp, tensor), weights, weights, weights, P()),
        out_specs=(P(), P()),
        check_vma=False,
    )
```

```python
import itertools

import jax
import jax.numpy as jnp
from jax import lax
from jax.experimental import pallas as pl
from jax.experimental.pallas import tpu as pltpu
from jax.sharding import Mesh, PartitionSpec as P

E = 6
HID = 28
PAD = 32
D = 4096
ROWS = 32
FEATS = 256
RING = 8
MIB = 1024 * 1024
VMEM = pl.BlockSpec(memory_space=pltpu.VMEM)
SMEM = pl.BlockSpec(memory_space=pltpu.SMEM)
HBM = pl.BlockSpec(memory_space=pltpu.HBM)
ALL = ("y", "zl", "c", "x", "zh")
OFFSETS = (0, -1, 1, -2, 2, -3, 3, 4)


def device(y, z, core, x):
    y, z = y % 8, z % 8
    return (((y * 2 + z % 2) * 2 + core) * 4 + x) * 4 + z // 2


PLACES = tuple(itertools.product(range(8), range(8), range(2), range(4)))


def shift(block, whose, step):
    pairs = []
    for y, z, core, x in PLACES:
        go = step if core == 0 else -step
        along_y = (core == 0) == (whose == "own")
        to = (y + go, z, core, x) if along_y else (y, z + go, core, x)
        pairs.append((device(y, z, core, x), device(*to)))
    return lax.ppermute(block, ALL, pairs)


def swap_cores(block):
    return lax.ppermute(block, "c", [(0, 1), (1, 0)])


def plane_groups():
    first = [
        [device(y, zl + 2 * zh, 0, x) for zl in range(2) for x in range(4) for zh in range(4)]
        for y in range(8)
    ]
    second = [[device(y, z, 1, x) for x in range(4) for y in range(8)] for z in range(8)]
    return first + second


def rings(own, theirs):
    own_fore = own_back = own
    their_fore = their_back = theirs
    own_blocks, their_blocks = [own], [theirs]
    for _ in range(RING // 2 - 1):
        own_fore, own_back = shift(own_fore, "own", 1), shift(own_back, "own", -1)
        their_back, their_fore = shift(their_back, "theirs", -1), shift(their_fore, "theirs", 1)
        own_fore, own_back = lax.optimization_barrier((own_fore, own_back))
        their_back, their_fore = lax.optimization_barrier((their_back, their_fore))
        own_blocks += [own_fore, own_back]
        their_blocks += [their_fore, their_back]
    own_blocks.append(shift(own_fore, "own", 1))
    their_blocks.append(shift(their_fore, "theirs", 1))
    return own_blocks, their_blocks


DIMS = (((1,), (1,)), ((), ()))
LAST = RING - 1


def pad_kernel(*refs):
    out_ref, done_ref = refs[3:]
    done_ref[...] = jnp.zeros(done_ref.shape, jnp.float32)
    for m in range(3):
        for e in range(E):
            out_ref[m, e, 16:PAD, :] = jnp.zeros((PAD - 16, D), jnp.bfloat16)
            out_ref[m, e, 0:HID, :] = refs[m][e]


def pad_rows(weights):
    return pl.pallas_call(
        pad_kernel,
        out_shape=(jax.ShapeDtypeStruct((3, E, PAD, D), jnp.bfloat16), jax.ShapeDtypeStruct((8, 128), jnp.float32)),
        in_specs=[VMEM] * 3,
        out_specs=(VMEM, VMEM),
        compiler_params=pltpu.CompilerParams(vmem_limit_bytes=11 * MIB),
        cost_estimate=pl.CostEstimate(flops=0, bytes_accessed=9 * MIB, transcendentals=0),
    )(*weights)


def split_kernel(plane_ref, mine_done_ref, other_done_ref, own_ref, their_ref):
    own_ref[...] = plane_ref[:, 0]
    their_ref[...] = plane_ref[:, 1]


def split(plane, *done):
    half = jax.ShapeDtypeStruct((32, ROWS, FEATS), jnp.bfloat16)
    return pl.pallas_call(
        split_kernel,
        out_shape=(half, half),
        in_specs=[VMEM] * 3,
        out_specs=(VMEM, VMEM),
        compiler_params=pltpu.CompilerParams(vmem_limit_bytes=3 * MIB),
    )(plane, *done)


def ring_place(mine, sign, offset):
    return lax.rem(mine + sign * offset + RING, RING)


def fill_tokens(tok_ref, blocks):
    for zl in range(2):
        for k in range(LAST):
            for t in range(16):
                tok_ref[zl, k * ROWS:(k + 1) * ROWS, t * FEATS:(t + 1) * FEATS] = blocks[k][zl * 16 + t]
        tok_ref[zl, LAST * ROWS:, :] = jnp.zeros((ROWS, D), jnp.bfloat16)


def fill_cotangents(cot_ref, blocks, my_z, sign, places):
    for j in range(LAST):
        z = ring_place(my_z, sign, OFFSETS[j])
        for x in range(4):
            for k in range(RING):
                cot_ref[z, k * ROWS:(k + 1) * ROWS, x * FEATS:(x + 1) * FEATS] = blocks[j][x * 8 + places[k]]
    cot_ref[ring_place(my_z, sign, OFFSETS[LAST])] = jnp.zeros((256, 4 * FEATS), jnp.bfloat16)


def weight_rows(w_ref, m):
    return w_ref[m].reshape(2 * E * PAD, D)


def down_rows_of(w_ref, zh):
    lanes = [pl.ds(pl.multiple_of((x * 4 + zh) * FEATS, FEATS), FEATS) for x in range(4)]
    return jnp.concatenate([w_ref[2, :, :, :, at] for at in lanes], axis=-1).reshape(2 * E * PAD, 4 * FEATS)


def middle_kernel(place_ref, mine_ref, other_ref, *refs):
    own, theirs = refs[:LAST], refs[LAST:2 * LAST]
    acc_ref, w_ref, tok_ref, cot_ref, sems = refs[2 * LAST:]
    my_y, my_z, sign = place_ref[0], place_ref[1], place_ref[2]
    copies = [
        [
            pltpu.make_async_copy(source.at[m], w_ref.at[m, p], sems.at[m, p])
            for p, source in enumerate((mine_ref, other_ref))
        ]
        for m in range(3)
    ]
    for pair in copies:
        for copy in pair:
            copy.start()
    places = [ring_place(my_y, sign, OFFSETS[k]) for k in range(RING)]

    @pl.when(sign > 0)
    def _():
        fill_tokens(tok_ref, own)
        fill_cotangents(cot_ref, theirs, my_z, sign, places)

    @pl.when(sign < 0)
    def _():
        fill_tokens(tok_ref, theirs)
        fill_cotangents(cot_ref, own, my_z, sign, places)

    for m in range(2):
        for copy in copies[m]:
            copy.wait()
        rows = weight_rows(w_ref, m)
        for zl in range(2):
            got = lax.dot_general(rows, tok_ref[zl], DIMS, preferred_element_type=jnp.float32)
            acc_ref[m, zl] = got.reshape(2 * E, PAD, 256)
    for copy in copies[2]:
        copy.wait()
    for zl in range(2):
        total = None
        for zh in range(4):
            rows = down_rows_of(w_ref, zh)
            got = lax.dot_general(rows, cot_ref[zh * 2 + zl], DIMS, preferred_element_type=jnp.float32)
            total = got if total is None else total + got
        acc_ref[2, zl] = total.reshape(2 * E, PAD, 256)


def tail_kernel(place_ref, logits_ref, w_ref, acc_ref, own_ref, their_ref, out_ref, tok_ref, cot_ref, late_ref, back_ref):
    my_y, my_z, sign = place_ref[0], place_ref[1], place_ref[2]
    places = [ring_place(my_y, sign, OFFSETS[k]) for k in range(RING)]
    last_z = ring_place(my_z, sign, OFFSETS[LAST])

    def fill(a_ref, b_ref):
        for zl in range(2):
            for t in range(16):
                tok_ref[zl * 128 + 96:(zl + 1) * 128, t * FEATS:(t + 1) * FEATS] = a_ref[zl * 16 + t]
        for x in range(4):
            for k in range(RING):
                cot_ref[k * ROWS:(k + 1) * ROWS, x * FEATS:(x + 1) * FEATS] = b_ref[x * 8 + places[k]]

    for zl in range(2):
        tok_ref[zl * 128:zl * 128 + 96, :] = jnp.zeros((96, D), jnp.bfloat16)

    @pl.when(sign > 0)
    def _():
        fill(own_ref, their_ref)

    @pl.when(sign < 0)
    def _():
        fill(their_ref, own_ref)

    for m in range(2):
        rows = weight_rows(w_ref, m)
        got = lax.dot_general(rows, tok_ref[...], DIMS, preferred_element_type=jnp.float32)
        late_ref[m] = got.reshape(2 * E, PAD, 256)
    rows = down_rows_of(w_ref, last_z // 2)
    got = lax.dot_general(rows, cot_ref[...], DIMS, preferred_element_type=jnp.float32)
    back_ref[lax.rem(last_z, 2)] = got.reshape(2 * E, PAD, 256)
    back_ref[1 - lax.rem(last_z, 2)] = jnp.zeros((2 * E, PAD, 256), jnp.float32)

    lane = lax.broadcasted_iota(jnp.int32, (8, 128), 1)
    seg = lax.broadcasted_iota(jnp.int32, (8, 128), 0)
    belongs = []
    for half in range(2):
        lane_seg = jnp.zeros((8, 128), jnp.int32)
        for k in range(4):
            lane_seg = jnp.where(lane // ROWS == k, places[half * 4 + k], lane_seg)
        belongs.append(lane_seg == seg)
    mixing = softmax_rows(logits_ref[...])

    token_sums = []
    for half in range(2):
        lanes = slice(half * 128, (half + 1) * 128)
        mix = [
            jnp.sum(jnp.where(belongs[half], mixing[:, e:e + 1], 0.0), axis=0, keepdims=True) for e in range(E)
        ]
        sums = [jnp.zeros((8, 128), jnp.float32) for _ in range(E)]
        for zl in range(2):
            late = slice(zl * 128, (zl + 1) * 128)

            def add(i, sums, zl=zl, lanes=lanes, late=late, mix=mix, half=half):
                pair, rows = (i // 4) * E, pl.ds((i % 4) * 8, 8)
                gate = [acc_ref[0, zl, pair + e, rows, lanes] for e in range(E)]
                up = [acc_ref[1, zl, pair + e, rows, lanes] for e in range(E)]
                if half == 1:
                    gate = [g + late_ref[0, pair + e, rows, late] for e, g in enumerate(gate)]
                    up = [u + late_ref[1, pair + e, rows, late] for e, u in enumerate(up)]
                back = [acc_ref[2, zl, pair + e, rows, lanes] + back_ref[zl, pair + e, rows, lanes] for e in range(E)]
                gate_sum = sum(mix[e] * gate[e] for e in range(E))
                upward = sum(mix[e] * up[e] for e in range(E))
                backward = sum(mix[e] * back[e] for e in range(E))
                sigmoid = jax.nn.sigmoid(gate_sum)
                active = gate_sum * sigmoid
                hidden = active * upward
                grad_gate = backward * upward * sigmoid * (1.0 + gate_sum * (1.0 - sigmoid))
                grad_up = backward * active
                return [
                    sums[e] + (grad_gate * gate[e] + grad_up * up[e] + hidden * back[e]) for e in range(E)
                ]

            for i in range(8):
                sums = add(i, sums)
        token_sums.append([jnp.sum(sums[e], axis=0, keepdims=True) for e in range(E)])
    out = jnp.zeros((8, 128), jnp.float32)
    for e in range(E):
        picked = sum(jnp.where(belongs[half], token_sums[half][e], 0.0) for half in range(2))
        out = jnp.where(lane == e, jnp.sum(picked, axis=1, keepdims=True), out)
    out_ref[...] = jnp.broadcast_to(out[None], out_ref.shape)


def softmax_rows(logits):
    raised = jnp.exp(logits - jnp.max(logits, axis=-1, keepdims=True))
    return raised / jnp.sum(raised, axis=-1, keepdims=True)


def add_kernel(got_ref, out_ref):
    out_ref[...] = jnp.broadcast_to(jnp.sum(got_ref[...], axis=0)[None], out_ref.shape)


def finish_kernel(got_ref, logits_ref, merge_ref, router_ref):
    merge_grad = jnp.sum(got_ref[...], axis=0)[:, :E]
    mixing = softmax_rows(logits_ref[...])
    merge_ref[...] = merge_grad
    router_ref[...] = mixing * (
        merge_grad - jnp.sum(mixing * merge_grad, axis=-1, keepdims=True)
    )


def on_device(tokens, cotangent, gate_rows, up_rows, down_rows, router_logits):
    my_y = lax.axis_index("y")
    my_z = lax.axis_index("zh") * 2 + lax.axis_index("zl")
    core = lax.axis_index("c")
    sign = 1 - 2 * core
    place = jnp.stack([my_y, my_z, sign]).astype(jnp.int32)
    place, *mine = lax.optimization_barrier((place, gate_rows, up_rows, down_rows))
    keep = jnp.where(core == 0, tokens, cotangent)
    got = swap_cores(jnp.where(core == 0, cotangent, tokens))
    pair = jnp.stack([keep, got])
    plane = lax.all_to_all(
        jnp.broadcast_to(pair[None], (32,) + pair.shape), ALL, 0, 0, axis_index_groups=plane_groups()
    )
    other = [swap_cores(w) for w in mine]
    mine = [pltpu.with_memory_space_constraint(w, pltpu.HBM) for w in mine]
    (mine, mine_done), (other, other_done) = pad_rows(mine), pad_rows(other)
    own, give = split(plane, mine_done, other_done)
    own_blocks, their_blocks = rings(own, swap_cores(give))

    acc_shape = (3, 2, 2 * E, PAD, 256)
    mine, other = (pltpu.with_memory_space_constraint(w, pltpu.HBM) for w in (mine, other))
    acc, weights = pl.pallas_call(
        middle_kernel,
        out_shape=(
            jax.ShapeDtypeStruct(acc_shape, jnp.float32),
            pltpu.VMEM((3, 2, E, PAD, D), jnp.bfloat16),
        ),
        in_specs=[SMEM, HBM, HBM] + [VMEM] * (2 * LAST),
        out_specs=(VMEM, VMEM),
        scratch_shapes=[
            pltpu.VMEM((2, 256, D), jnp.bfloat16),
            pltpu.VMEM((8, 256, 4 * FEATS), jnp.bfloat16),
            pltpu.SemaphoreType.DMA((3, 2)),
        ],
        compiler_params=pltpu.CompilerParams(vmem_limit_bytes=14 * MIB),
        cost_estimate=pl.CostEstimate(flops=9_000_000_000, bytes_accessed=24 * MIB, transcendentals=0),
    )(place, mine, other, *own_blocks[:LAST], *their_blocks[:LAST])
    part = pl.pallas_call(
        tail_kernel,
        out_shape=jax.ShapeDtypeStruct((32, 8, 128), jnp.float32),
        in_specs=[SMEM] + [VMEM] * 5,
        out_specs=VMEM,
        scratch_shapes=[
            pltpu.VMEM((256, D), jnp.bfloat16),
            pltpu.VMEM((256, 4 * FEATS), jnp.bfloat16),
            pltpu.VMEM((2, 2 * E, PAD, 256), jnp.float32),
            pltpu.VMEM((2, 2 * E, PAD, 256), jnp.float32),
        ],
        compiler_params=pltpu.CompilerParams(vmem_limit_bytes=8 * MIB),
    )(place, router_logits, weights, acc, own_blocks[LAST], their_blocks[LAST])
    got = lax.all_to_all(part, ("x", "y"), 0, 0)
    part = pl.pallas_call(
        add_kernel,
        out_shape=jax.ShapeDtypeStruct((16, 8, 128), jnp.float32),
        in_specs=[VMEM],
        out_specs=VMEM,
        compiler_params=pltpu.CompilerParams(vmem_limit_bytes=2 * MIB),
    )(got)
    got = lax.all_to_all(part, ("zl", "zh", "c"), 0, 0)
    small = jax.ShapeDtypeStruct((8, E), jnp.float32)
    return pl.pallas_call(
        finish_kernel,
        out_shape=(small, small),
        in_specs=[VMEM, VMEM],
        out_specs=(VMEM, VMEM),
        compiler_params=pltpu.CompilerParams(vmem_limit_bytes=2 * MIB),
    )(got, router_logits)


def solution(mesh):
    fine = Mesh(mesh.devices.reshape(8, 2, 2, 4, 4), ("y", "zl", "c", "x", "zh"))
    dp, tensor = ("y", "zl", "c"), ("x", "zh")
    weights = P(None, dp + tensor, None)
    return jax.shard_map(
        on_device,
        mesh=fine,
        in_specs=(P(dp, tensor), P(dp, tensor), weights, weights, weights, P()),
        out_specs=(P(), P()),
        check_vma=False,
    )
```
